256 devices in a mesh: batch: 128 (over x_lo, z, y, core), mp: 2 (over x_hi).
Axes of the slice: x: 4 (x_hi: 2, x_lo: 2; x = x_hi * 2 + x_lo), y: 4, z: 8, core: 2. Of those that a mesh axis runs over, the one named last changes fastest.
Arguments:
- image_feats: bfloat16 [98304, 1152], P('batch'), may hold values from -24 to 24
- text_feats: bfloat16 [98304, 1152], P('batch'), may hold values from -24 to 24
- image_head: bfloat16 [1152, 1152], P('batch', 'mp'), may hold values from -0.1875 to 0.1875
- text_head: bfloat16 [1152, 1152], P('batch', 'mp'), may hold values from -0.1875 to 0.1875
- positive: int32 [128, 768], P('batch'), may hold values from 0 to 767, each once within a row
- logit_scale: float32 [1], replicated, may hold values from 20 to 40
- logit_bias: float32 [1], replicated, may hold values from -3 to -1
Outputs:
- image_head_grad: float32 [1152, 1152], P('batch', 'mp')
- text_head_grad: float32 [1152, 1152], P('batch', 'mp')
The draws below stay inside these ranges and needn't reach their ends.
Inputs may be any that keep to these rules, and one draw needn't show every extreme that they name: Each row of positive holds every number of 0 to 767 once.
All inputs are finite; a program needn't handle non-finite values.
Results may differ from the reference program's by a relative error of at most 0.00205.
Values may be sent and summed in bfloat16 or wider, within the bound.
No kernel may reach another device: no remote copies, remote signals or barrier semaphores. Data moves between devices by JAX's collectives and lax.ppermute only.
A program may use at most 64 MiB of HBM per device.

```python
import jax
import jax.numpy as jnp
from jax import lax

F = 1152
E = 1152
TOK_DEV = 768
BLOCKS = 128
TOKENS = 98304


def strengthened(values, own_key, source, target, parts, factor):
    def block_of(position):
        return (jnp.arange(values.shape[position]) // (values.shape[position] // parts)).reshape((-1,) + (1,) * (values.ndim - 1 - position))

    near = jax.random.permutation(own_key, parts)[block_of(target)]
    other_side = (block_of(target) + parts // 2) % parts
    return jnp.where((block_of(source) == near) | (block_of(source) == other_side), factor * values, values)


def level_of(stream_key, shape, shards, smallest, high):
    def one(dim, blocks):
        heights = jax.random.uniform(jax.random.fold_in(jax.random.fold_in(stream_key, 6), dim), (blocks,), jnp.float32, smallest / len(shards), high / len(shards))
        return jnp.repeat(jnp.exp(heights), shape[dim] // blocks).reshape((-1,) + (1,) * (len(shape) - dim - 1))

    level = one(*shards[0])
    for cut in shards[1:]:
        level = level * one(*cut)
    return level


def gaussian(own_key, shape, width, limit, cuts=(), held_as=jnp.bfloat16):
    level = level_of(own_key, shape, cuts, -0.22, 0.18) if cuts else 1.0
    values = jax.random.normal(own_key, shape, jnp.float32) * width * level
    return jnp.minimum(jnp.maximum(values, -limit), limit).astype(held_as)


def gaussian_with(stream_key, shape, spread, reach, split, heavy, kind=jnp.bfloat16):
    result = spread * jax.random.normal(stream_key, shape, jnp.float32)
    if split:
        result = result * level_of(stream_key, shape, split, -0.22, 0.18)
    return jnp.clip(strengthened(result, jax.random.fold_in(stream_key, 3), *heavy), -reach, reach).astype(kind)


def setup_inputs(seed: int = 0) -> dict:
    streams_of = jax.random.split(jax.random.key(seed), 8)
    image_feats = gaussian_with(streams_of[0], (TOKENS, F), 1.0, 24.0, ((0, 128),), (0, 1, 128, 5.5))
    text_feats = gaussian_with(streams_of[1], (TOKENS, F), 1.0, 24.0, ((0, 128),), (0, 1, 128, 5.5))
    image_head = gaussian(streams_of[2], (F, E), F ** -0.5, 0.1875, ((0, 128), (1, 2)))
    text_head = gaussian(streams_of[3], (F, E), F ** -0.5, 0.1875, ((0, 128), (1, 2)))
    positive = jax.vmap(lambda own: jax.random.permutation(own, TOK_DEV))(jax.random.split(streams_of[4], BLOCKS)).reshape((BLOCKS, TOK_DEV)).astype(jnp.int32)
    logit_scale = jnp.clip(jax.random.uniform(streams_of[5], (1,), jnp.float32, 20.0, 40.0), 20.0, 40.0)
    logit_bias = jnp.clip(jax.random.uniform(streams_of[6], (1,), jnp.float32, -3.0, -1.0), -3.0, -1.0)
    return dict(image_feats=image_feats, text_feats=text_feats, image_head=image_head, text_head=text_head, positive=positive, logit_scale=logit_scale, logit_bias=logit_bias)


EPS = 1e-06
LOSS_SHARE = 0.0625

def normalize(raw):
    length = jnp.sqrt(lax.optimization_barrier(jnp.sum(raw * raw, axis=1, keepdims=True)) + EPS)
    return (raw / length, length)

def coefficient(scores, sign, scale, offset):
    logit = scale * scores + offset
    return (-sign * scale * jax.nn.sigmoid(-sign * logit) * LOSS_SHARE).astype(jnp.bfloat16)

def reference(image_feats, text_feats, image_head, text_head, positive, logit_scale, logit_bias):
    scale = logit_scale[0]
    offset = logit_bias[0]
    image_raw = jnp.dot(image_feats, image_head, preferred_element_type=jnp.float32)
    text_raw = jnp.dot(text_feats, text_head, preferred_element_type=jnp.float32)
    image_unit, image_len = normalize(image_raw)
    text_unit, text_len = normalize(text_raw)
    image_emb = image_unit.astype(jnp.bfloat16).astype(jnp.float32).reshape(BLOCKS, TOK_DEV, E)
    text_emb = text_unit.astype(jnp.bfloat16).astype(jnp.float32).reshape(BLOCKS, TOK_DEV, E)
    text_prev = jnp.roll(text_emb, 1, axis=0)
    scores_own = jnp.einsum('bre,bqe->brq', image_emb, text_emb)
    scores_prev = jnp.einsum('bre,bqe->brq', image_emb, text_prev)
    columns = jnp.arange(TOK_DEV, dtype=jnp.int32)
    sign_own = jnp.where(columns[None, None, :] == positive[:, :, None], 1.0, -1.0).astype(jnp.float32)
    coef_own = coefficient(scores_own, sign_own, scale, offset).astype(jnp.float32)
    coef_prev = coefficient(scores_prev, jnp.float32(-1.0), scale, offset).astype(jnp.float32)
    image_grad = jnp.einsum('brq,bqe->bre', coef_own, text_emb) + jnp.einsum('brq,bqe->bre', coef_prev, text_prev)
    lent = jnp.einsum('brq,bre->bqe', coef_prev, image_emb)
    text_grad = jnp.einsum('brq,bre->bqe', coef_own, image_emb) + jnp.roll(lent, -1, axis=0)
    image_grad = image_grad.reshape(TOKENS, E)
    text_grad = text_grad.reshape(TOKENS, E)
    image_rad = lax.optimization_barrier(jnp.sum(image_unit * image_grad, axis=1, keepdims=True))
    text_rad = lax.optimization_barrier(jnp.sum(text_unit * text_grad, axis=1, keepdims=True))
    image_raw_grad = ((image_grad - image_unit * image_rad) / image_len).astype(jnp.bfloat16)
    text_raw_grad = ((text_grad - text_unit * text_rad) / text_len).astype(jnp.bfloat16)
    dims = (((0,), (0,)), ((), ()))
    image_head_grad = lax.dot_general(image_feats, image_raw_grad, dims, preferred_element_type=jnp.float32)
    text_head_grad = lax.dot_general(text_feats, text_raw_grad, dims, preferred_element_type=jnp.float32)
    return (image_head_grad, text_head_grad)
```

```python
import functools

import jax
import jax.numpy as jnp
import numpy as np
from jax import lax
from jax.experimental import pallas as pl
from jax.experimental.pallas import tpu as pltpu
from jax.sharding import Mesh
from jax.sharding import PartitionSpec as P

EPS = 1e-06
LOSS_SHARE = 0.0625
BF = jnp.bfloat16
F32 = jnp.float32

NAMES = ("xl", "z1", "z2", "y", "c", "m")
SIZES = (2, 2, 4, 4, 2, 2)
X = ("xl", "m")
Z = ("z1", "z2")
W = 576
HW = 640
EW = 2 * HW
F = 1152
TOK = 768
RA, RC = 64, 80
TM = 256


def _head_order():
    k = np.arange(F)
    block, r = k // 144, k % 144
    xl, z2 = block // 4, block % 4
    y, z1, c, i = r // 36, (r % 36) // 18, (r % 18) // 9, r % 9
    return ((((xl * 2 + z1) * 4 + z2) * 4 + y) * 2 + c) * 9 + i


def _grad_order():
    s = np.arange(F // 2)
    xl, y, z, i = s // 288, (s % 288) // 72, (s % 72) // 9, s % 9
    return (((xl * 8 + z) * 4 + y) * 2) * 9 + i


def shift_x(v, by):
    def place(q):
        return (q % 2) * 2 + q // 2

    return lax.ppermute(v, X, [(place(i), place((i + by) % 4)) for i in range(4)])


def shift(v, axis, by):
    n = lax.axis_size(axis)
    return lax.ppermute(v, axis, [(i, (i + by) % n) for i in range(n)])


def to_neighbour(v):
    pairs = [(b * 2 + m, ((b + 1 - 2 * m) % 128) * 2 + m) for b in range(128) for m in range(2)]
    return lax.ppermute(v, NAMES, pairs)


def in_order(mine, other, index):
    return jnp.where(
        index == 0, jnp.concatenate([mine, other], 0), jnp.concatenate([other, mine], 0)
    )


def tower_kernel(*refs):
    (par, a_hbm, b_hbm, n_hbm, rowkey, colkey) = refs[:6]
    pieces = refs[6:26]
    out = refs[26]
    heads, av, bv, unit, emb, bemb, inv, sem = refs[27:]
    m, c = lax.axis_index("m"), lax.axis_index("c")
    x = m * 2 + lax.axis_index("xl")
    z2 = lax.axis_index("z2")
    copies = [
        pltpu.make_async_copy(a_hbm, av, sem.at[0]),
        pltpu.make_async_copy(b_hbm, bv.at[pl.ds(0, TOK)], sem.at[1]),
        pltpu.make_async_copy(n_hbm, bv.at[pl.ds(TOK, TOK)], sem.at[2]),
    ]

    def put(src, row0, rows, head, dx, dz, part):
        xx = lax.rem(x + dx + 4, 4)
        zz = lax.rem(z2 + dz + 4, 4)
        half, xl = xx // 2, lax.rem(xx, 2)
        row = (xl * 4 + zz) * 144 + part
        copies.append(
            pltpu.make_async_copy(
                src.at[pl.ds(row0, rows)],
                heads.at[
                    head, pl.ds(pl.multiple_of(row, 16), rows), pl.ds(pl.multiple_of(half * HW, 128), HW)
                ],
                sem.at[len(copies)],
            )
        )

    steps = (0, -1, 1, 2)
    for group in range(2):
        head = c if group == 0 else 1 - c
        p = pieces[group * 10 : group * 10 + 10]
        for k, dx in enumerate(steps):
            for src, dz in ((p[0], 0), (p[1], -1), (p[2], 1)):
                put(src, k * RA, RA, head, dx, dz, 0)
            put(p[3] if k < 2 else p[4], (k % 2) * RA, RA, head, dx, 2, 0)
        for k, dz in enumerate(steps):
            for src, dx in ((p[5], 0), (p[6], -1), (p[7], 1)):
                put(src, k * RC, RC, head, dx, dz, RA)
            put(p[8] if k < 2 else p[9], (k % 2) * RC, RC, head, 2, dz, RA)
    for copy in copies:
        copy.start()
    for copy in copies:
        copy.wait()

    scale, offset = par[0], par[1]
    gain = scale * LOSS_SHARE

    @pl.loop(0, TOK // TM)
    def _(t):
        rows = pl.ds(pl.multiple_of(t * TM, TM), TM)
        raw = jnp.dot(av[rows], heads[m], preferred_element_type=F32)
        inv_len = 1.0 / jnp.sqrt(jnp.sum(raw * raw, axis=1, keepdims=True) + EPS)
        u = raw * inv_len
        unit[rows] = u
        emb[rows] = u.astype(BF)
        inv[rows] = jnp.broadcast_to(inv_len, (TM, 128))

    @pl.loop(0, 2 * TOK // TM)
    def _(t):
        rows = pl.ds(pl.multiple_of(t * TM, TM), TM)
        raw = jnp.dot(bv[rows], heads[1 - m], preferred_element_type=F32)
        inv_len = 1.0 / jnp.sqrt(jnp.sum(raw * raw, axis=1, keepdims=True) + EPS)
        bemb[rows] = (raw * inv_len).astype(BF)

    @pl.loop(0, TOK // TM)
    def _(t):
        rows = pl.ds(pl.multiple_of(t * TM, TM), TM)
        e = emb[rows]
        dims = (((1,), (1,)), ((), ()))
        own = lax.dot_general(e, bemb[:TOK], dims, preferred_element_type=F32) * scale + offset
        near = lax.dot_general(e, bemb[TOK:], dims, preferred_element_type=F32) * scale + offset
        hit = rowkey[rows] == colkey[...]
        own_coef = jnp.where(hit, -gain, gain) / (1.0 + jnp.exp(jnp.where(hit, own, -own)))
        near_coef = gain / (1.0 + jnp.exp(-near))
        grad = jnp.dot(own_coef.astype(BF), bemb[:TOK], preferred_element_type=F32) + jnp.dot(
            near_coef.astype(BF), bemb[TOK:], preferred_element_type=F32
        )
        u = unit[rows]
        radial = jnp.sum(u * grad, axis=1, keepdims=True)
        out[rows] = ((grad - u * radial) * inv[rows][:, :1]).astype(BF)


def tower(par, a, b, n, rowkey, colkey, pieces):
    any_ = pl.BlockSpec(memory_space=pl.ANY)
    vm = pl.BlockSpec(memory_space=pltpu.VMEM)
    return pl.pallas_call(
        tower_kernel,
        out_shape=jax.ShapeDtypeStruct((TOK, EW), BF),
        in_specs=[pl.BlockSpec(memory_space=pltpu.SMEM), any_, any_, any_, vm, vm] + [any_] * 20,
        out_specs=vm,
        scratch_shapes=[
            pltpu.VMEM((2, F, EW), BF),
            pltpu.VMEM((TOK, F), BF),
            pltpu.VMEM((2 * TOK, F), BF),
            pltpu.VMEM((TOK, EW), F32),
            pltpu.VMEM((TOK, EW), BF),
            pltpu.VMEM((2 * TOK, EW), BF),
            pltpu.VMEM((TOK, 128), F32),
            pltpu.SemaphoreType.DMA((67,)),
        ],
        compiler_params=pltpu.CompilerParams(vmem_limit_bytes=56 << 20),
        cost_estimate=pl.CostEstimate(
            flops=13_000_000_000, bytes_accessed=14_000_000, transcendentals=2_400_000
        ),
    )(par, a, b, n, rowkey, colkey, *pieces)


def gathered_pieces(image_head, text_head):
    c, z1, y = lax.axis_index("c"), lax.axis_index("z1"), lax.axis_index("y")
    pad = ((0, 0), (0, HW - W))
    mine = jnp.pad(jnp.where(c == 0, image_head, text_head), pad)
    theirs = jnp.pad(jnp.where(c == 0, text_head, image_head), pad)
    v = in_order(mine, shift(theirs, "c", 1), c)
    v = in_order(v, shift(v, "z1", 1), z1)
    got = [v, shift(v, "y", 1), shift(v, "y", -1), shift(v, "y", 2)]
    block = jnp.zeros((4, 36, HW), BF)
    for by, g in zip((0, 1, -1, 2), got):
        block = lax.dynamic_update_slice(block, g[None], ((y - by + 4) % 4, 0, 0))
    v = block.reshape(144, HW)
    a, d = v[:RA], v[RA:]
    a4 = jnp.concatenate([a, shift_x(a, 1), shift_x(a, -1), shift_x(a, 2)], 0)
    d4 = jnp.concatenate(
        [d, shift(d, Z, 1), shift(d, Z, -1), shift(d[:48], Z, 2), shift(d[48:], Z, -2)], 0
    )
    d_r, d_l = shift_x(d4, 1), shift_x(d4, -1)
    own = [
        a4,
        shift(a4, Z, 1),
        shift(a4, Z, -1),
        shift(a4[: 2 * RA], Z, 2),
        shift(a4[2 * RA :], Z, -2),
        d4,
        d_r,
        d_l,
        shift_x(d_r[: 2 * RC], 1),
        shift_x(d_l[2 * RC :], -1),
    ]
    return own + [shift(p, "c", 1) for p in own], got[3]


def local(image_feats, text_feats, image_head, text_head, positive, logit_scale, logit_bias):
    m, c = lax.axis_index("m"), lax.axis_index("c")
    par = jnp.concatenate([logit_scale, logit_bias])
    a = jnp.where(m == 0, image_feats, text_feats)
    b = jnp.where(m == 0, text_feats, image_feats)
    rows = lax.broadcasted_iota(jnp.int32, (F, F), 0)
    to_heads = (rows == jnp.asarray(_head_order(), jnp.int32)[None, :]).astype(BF)
    a_heads = jnp.dot(a, to_heads, preferred_element_type=F32).astype(BF)
    b_heads = jnp.dot(b, to_heads, preferred_element_type=F32).astype(BF)
    order = jnp.asarray(_grad_order(), jnp.int32)[None, :]

    def grad_rows(core):
        pick = (rows[:, : F // 2] == order + 9 * core).astype(BF)
        dims = (((0,), (1,)), ((), ()))
        return lax.dot_general(pick, a, dims, preferred_element_type=F32).astype(BF)

    at_own = grad_rows(c)
    at_other = shift(grad_rows(1 - c), "c", 1)

    pieces, started = gathered_pieces(image_head, text_head)
    b_sent, _ = lax.optimization_barrier((b_heads, started))
    n_heads = to_neighbour(b_sent)

    ident = lax.iota(jnp.int32, TOK)
    rowkey = jnp.where(m == 0, positive[0], ident)[:, None]
    colkey = jnp.where(m == 0, ident, positive[0])[None, :]
    grad = tower(par, a_heads, b_heads, n_heads, rowkey, colkey, pieces)

    grad_other = shift(grad, "c", 1)
    part = jnp.dot(at_own, grad, preferred_element_type=F32) + jnp.dot(
        at_other, grad_other, preferred_element_type=F32
    )
    part = part.astype(BF).reshape(8, 72, 2, HW).transpose(0, 2, 1, 3).reshape(16, 72, HW)
    part = lax.all_to_all(part, ("xl", "y", "m"), 0, 0, tiled=False)
    part = jnp.sum(part.reshape(8, 2, 72, HW).astype(F32), axis=0)
    part = part.reshape(2, 8, 9, HW).transpose(1, 0, 2, 3).reshape(8, 18, HW)
    part = lax.all_to_all(part, Z, 0, 0, tiled=False)
    part = jnp.sum(part, axis=0)
    return part[:9, :W], part[9:, :W]


def solution(mesh):
    parts = Mesh(mesh.devices.reshape(SIZES), NAMES)
    batch = ("xl", "z1", "z2", "y", "c")
    in_specs = (
        P(batch, None),
        P(batch, None),
        P(batch, "m"),
        P(batch, "m"),
        P(batch, None),
        P(),
        P(),
    )
    out_specs = (P(batch, "m"), P(batch, "m"))
    return jax.shard_map(local, mesh=parts, in_specs=in_specs, out_specs=out_specs, check_vma=False)
```

```python
import jax
import jax.numpy as jnp
import numpy as np
from jax import lax
from jax.experimental import pallas as pl
from jax.experimental.pallas import tpu as pltpu
from jax.sharding import Mesh
from jax.sharding import PartitionSpec as P

EPS = 1e-06
LOSS_SHARE = 0.0625
BF = jnp.bfloat16
F32 = jnp.float32

NAMES = ("xl", "z1", "z2", "y", "c", "m")
SIZES = (2, 2, 4, 4, 2, 2)
Z = ("z1", "z2")
W = 576
HW = 640
EW = 2 * HW
F = 1152
TOK = 768
TM = 384
ROWS = 144
STEPS = (0, -1, 1, 2)
CORE = ("xl", "z1", "z2", "c", "m")


def _head_order():
    k = np.arange(F)
    block, r = k // 144, k % 144
    xl, z2 = block // 4, block % 4
    y, z1, c, i = r // 36, (r % 36) // 18, (r % 18) // 9, r % 9
    return ((((xl * 2 + z1) * 4 + z2) * 4 + y) * 2 + c) * 9 + i


def _grad_order():
    s = np.arange(F // 2)
    xl, y, z, i = s // 288, (s % 288) // 72, (s % 72) // 9, s % 9
    return (((xl * 8 + z) * 4 + y) * 2) * 9 + i


def shift_xz(v, by, last):
    pairs = []
    for i in range(64):
        xl, z, c, m = i // 32, i // 4 % 8, i // 2 % 2, i % 2
        x = m * 2 + xl
        if (c == 0) != last:
            x = (x + by) % 4
        else:
            z = (z + by) % 8
        pairs.append((i, (((x % 2) * 8 + z) * 2 + c) * 2 + x // 2))
    return lax.ppermute(v, CORE, pairs)


def shift(v, axis, by):
    n = lax.axis_size(axis)
    return lax.ppermute(v, axis, [(i, (i + by) % n) for i in range(n)])


def to_neighbour(v):
    pairs = [(b * 2 + m, ((b + 1 - 2 * m) % 128) * 2 + m) for b in range(128) for m in range(2)]
    return lax.ppermute(v, NAMES, pairs)


def in_order(mine, other, index):
    return jnp.where(
        index == 0, jnp.concatenate([mine, other], 0), jnp.concatenate([other, mine], 0)
    )


NT = (((1,), (1,)), ((), ()))


def normalized(raw):
    inv_len = 1.0 / jnp.sqrt(jnp.sum(raw * raw, axis=1, keepdims=True) + EPS)
    return raw * inv_len, inv_len


def own_kernel(*refs):
    par, a_hbm, b_hbm, rowkey, colkey = refs[:5]
    pieces = refs[5:21]
    unit, emb, inv, part, head_out = refs[21:26]
    heads, av, bv, bemb, sem = refs[26:]
    m, c = lax.axis_index("m"), lax.axis_index("c")
    x = m * 2 + lax.axis_index("xl")
    z2 = lax.axis_index("z2")
    copies = [
        pltpu.make_async_copy(a_hbm, av, sem.at[0]),
        pltpu.make_async_copy(b_hbm, bv, sem.at[1]),
    ]

    def put(src, k, head, first, last):
        dx = jnp.where(head == 0, first, last)
        dz = jnp.where(head == 0, last, first)
        xx = lax.rem(x + dx + 4, 4)
        block = lax.rem(xx, 2) * 4 + lax.rem(z2 + dz + 4, 4)
        copies.append(
            pltpu.make_async_copy(
                src.at[pl.ds(k * ROWS, ROWS)],
                heads.at[
                    head,
                    pl.ds(pl.multiple_of(block * ROWS, 16), ROWS),
                    pl.ds(pl.multiple_of((xx // 2) * HW, 128), HW),
                ],
                sem.at[len(copies)],
            )
        )

    for group in range(2):
        head = c if group == 0 else 1 - c
        for k, last in enumerate((0, -1, 1, 2)):
            near, far = pieces[group * 8 + 2 * k : group * 8 + 2 * k + 2]
            for i, first in enumerate(STEPS):
                put(near if i < 2 else far, i % 2, head, first, last)
    for copy in copies:
        copy.start()
    for copy in copies:
        copy.wait()
    save = pltpu.make_async_copy(heads.at[1 - m], head_out, sem.at[len(copies)])
    save.start()

    scale, offset = par[0], par[1]
    gain = scale * LOSS_SHARE
    for t in range(2):
        rows = pl.ds(t * TM, TM)
        u, inv_len = normalized(jnp.dot(av[rows], heads[m], preferred_element_type=F32))
        unit[rows] = u
        emb[rows] = u.astype(BF)
        inv[rows] = jnp.broadcast_to(inv_len, (TM, 128))
    for t in range(2):
        rows = pl.ds(t * TM, TM)
        u, _ = normalized(jnp.dot(bv[rows], heads[1 - m], preferred_element_type=F32))
        bemb[rows] = u.astype(BF)
    for t in range(2):
        rows = pl.ds(t * TM, TM)
        logit = lax.dot_general(emb[rows], bemb[...], NT, preferred_element_type=F32) * scale + offset
        hit = rowkey[rows] == colkey[...]
        coef = jnp.where(hit, -gain, gain) / (1.0 + jnp.exp(jnp.where(hit, logit, -logit)))
        part[rows] = jnp.dot(coef.astype(BF), bemb[...], preferred_element_type=F32)
    save.wait()


def near_kernel(par, n_hbm, head_hbm, unit, emb, inv, part, out, nv, head, nemb, sem):
    loads = [
        pltpu.make_async_copy(n_hbm, nv, sem.at[0]),
        pltpu.make_async_copy(head_hbm, head, sem.at[1]),
    ]
    for load in loads:
        load.start()
    for load in loads:
        load.wait()
    scale, offset = par[0], par[1]
    gain = scale * LOSS_SHARE
    for t in range(2):
        rows = pl.ds(t * TM, TM)
        u, _ = normalized(jnp.dot(nv[rows], head[...], preferred_element_type=F32))
        nemb[rows] = u.astype(BF)
    for t in range(2):
        rows = pl.ds(t * TM, TM)
        logit = lax.dot_general(emb[rows], nemb[...], NT, preferred_element_type=F32) * scale + offset
        coef = gain / (1.0 + jnp.exp(-logit))
        grad = part[rows] + jnp.dot(coef.astype(BF), nemb[...], preferred_element_type=F32)
        u = unit[rows]
        radial = jnp.sum(u * grad, axis=1, keepdims=True)
        out[rows] = ((grad - u * radial) * inv[rows][:, :1]).astype(BF)


ANY = pl.BlockSpec(memory_space=pl.ANY)
VM = pl.BlockSpec(memory_space=pltpu.VMEM)
SM = pl.BlockSpec(memory_space=pltpu.SMEM)


def hbm(v):
    return pltpu.with_memory_space_constraint(v, pltpu.HBM)


def vmem(v):
    return pltpu.with_memory_space_constraint(v, pltpu.VMEM)


def own_pair(par, a, b, rowkey, colkey, pieces):
    return pl.pallas_call(
        own_kernel,
        out_shape=(
            pltpu.VMEM((TOK, EW), F32),
            pltpu.VMEM((TOK, EW), BF),
            pltpu.VMEM((TOK, 128), F32),
            pltpu.VMEM((TOK, EW), F32),
            pltpu.HBM((F, EW), BF),
        ),
        in_specs=[SM, ANY, ANY, VM, VM] + [ANY] * 16,
        out_specs=(VM, VM, VM, VM, ANY),
        scratch_shapes=[
            pltpu.VMEM((2, F, EW), BF),
            pltpu.VMEM((TOK, F), BF),
            pltpu.VMEM((TOK, F), BF),
            pltpu.VMEM((TOK, EW), BF),
            pltpu.SemaphoreType.DMA((35,)),
        ],
        compiler_params=pltpu.CompilerParams(vmem_limit_bytes=30 << 20),
        cost_estimate=pl.CostEstimate(flops=7_500_000_000, bytes_accessed=23_000_000, transcendentals=1_200_000),
    )(par, hbm(a), hbm(b), rowkey, colkey, *[hbm(p) for p in pieces])


def near_pair(par, n, head, unit, emb, inv, part):
    return pl.pallas_call(
        near_kernel,
        out_shape=jax.ShapeDtypeStruct((TOK, EW), BF),
        in_specs=[SM, ANY, ANY, VM, VM, VM, VM],
        out_specs=VM,
        scratch_shapes=[
            pltpu.VMEM((TOK, F), BF),
            pltpu.VMEM((F, EW), BF),
            pltpu.VMEM((TOK, EW), BF),
            pltpu.SemaphoreType.DMA((2,)),
        ],
        compiler_params=pltpu.CompilerParams(vmem_limit_bytes=24 << 20),
        cost_estimate=pl.CostEstimate(flops=5_300_000_000, bytes_accessed=7_000_000, transcendentals=1_200_000),
    )(par, hbm(n), hbm(head), vmem(unit), vmem(emb), vmem(inv), vmem(part))


def first_sum_kernel(at, grad, out):
    @pl.loop(0, 2)
    def _(t):
        rows = pl.ds(pl.multiple_of(t * 288, 288), 288)
        out[rows] = jnp.dot(at[rows], grad[...], preferred_element_type=F32)


def second_sum_kernel(at, grad, part, out):
    @pl.loop(0, 2)
    def _(t):
        rows = pl.ds(pl.multiple_of(t * 288, 288), 288)
        total = part[rows] + jnp.dot(at[rows], grad[...], preferred_element_type=F32)
        for k in range(4):
            for half in range(2):
                out[t * 8 + k * 2 + half] = total[
                    k * 72 : (k + 1) * 72, half * HW : (half + 1) * HW
                ].astype(BF)


def first_sum(at, grad):
    return pl.pallas_call(
        first_sum_kernel,
        out_shape=jax.ShapeDtypeStruct((F // 2, EW), F32),
        compiler_params=pltpu.CompilerParams(vmem_limit_bytes=24 << 20),
        cost_estimate=pl.CostEstimate(flops=1_132_462_080, bytes_accessed=5_800_000, transcendentals=0),
    )(at, grad)


def second_sum(at, grad, part):
    return pl.pallas_call(
        second_sum_kernel,
        out_shape=jax.ShapeDtypeStruct((16, 72, HW), BF),
        compiler_params=pltpu.CompilerParams(vmem_limit_bytes=24 << 20),
        cost_estimate=pl.CostEstimate(flops=1_132_462_080, bytes_accessed=7_000_000, transcendentals=0),
    )(at, grad, part)


def after(value, *others):
    return lax.optimization_barrier((value, *others))[0]


def local(image_feats, text_feats, image_head, text_head, positive, logit_scale, logit_bias):
    m, c = lax.axis_index("m"), lax.axis_index("c")
    z1, y = lax.axis_index("z1"), lax.axis_index("y")

    image_other, text_other = shift(image_head, "c", 1), shift(text_head, "c", 1)
    v = jnp.where(
        c == 0,
        jnp.concatenate([image_head, image_other], 0),
        jnp.concatenate([text_other, text_head], 0),
    )
    v = jnp.pad(in_order(v, shift(v, "z1", 1), z1), ((0, 0), (0, HW - W)))
    got = [v, shift(v, "y", 1), shift(v, "y", -1), shift(v, "y", 2)]
    (images, texts), got = lax.optimization_barrier(((image_feats, text_feats), got))
    v = jnp.zeros((4, 36, HW), BF)
    for by, g in zip((0, 1, -1, 2), got):
        v = lax.dynamic_update_slice(v, g[None], ((y - by + 4) % 4, 0, 0))
    v = v.reshape(ROWS, HW)

    rows = lax.broadcasted_iota(jnp.int32, (F, F), 0)
    to_heads = (rows == jnp.asarray(_head_order(), jnp.int32)[None, :]).astype(BF)
    a = jnp.where(m == 0, images, texts)
    a_heads = jnp.dot(a, to_heads, preferred_element_type=F32).astype(BF)
    lo = jnp.concatenate([v, shift_xz(v, 1, False)], 0)
    far, a_heads = lax.optimization_barrier((shift_xz(v, 2, False), a_heads))
    hi = jnp.concatenate([shift_xz(v, -1, False), far], 0)
    images, texts = after((image_feats, text_feats), hi)
    b = jnp.where(m == 0, texts, images)
    b_heads = jnp.dot(b, to_heads, preferred_element_type=F32).astype(BF)
    lo_left, hi_right = shift_xz(lo, 1, True), shift_xz(hi, -1, True)
    hi_left, lo_right = shift_xz(hi, 1, True), shift_xz(lo, -1, True)
    (lo_left, hi_right), b_heads = lax.optimization_barrier(((lo_left, hi_right), b_heads))
    lo_far, hi_far = shift_xz(lo_left, 1, True), shift_xz(hi_right, -1, True)
    par = jnp.concatenate([logit_scale, logit_bias])
    ident = lax.iota(jnp.int32, TOK)
    rowkey = jnp.where(m == 0, positive[0], ident)[:, None]
    colkey = jnp.where(m == 0, ident, positive[0])[None, :]
    lo, par, rowkey, colkey = lax.optimization_barrier((lo, par, rowkey, colkey))
    own = [lo, hi, lo_left, hi_left, lo_right, hi_right, lo_far, hi_far]
    pieces = own + [shift(p, "c", 1) for p in own]

    b_heads, _ = lax.optimization_barrier((b_heads, (lo_far, hi_far)))
    n_heads = to_neighbour(b_heads)
    unit, emb, inv, part, head = own_pair(par, a_heads, b_heads, rowkey, colkey, pieces)

    a = after(a, emb)
    order = jnp.asarray(_grad_order(), jnp.int32)[None, :]

    def grad_rows(core):
        pick = (rows[:, : F // 2] == order + 9 * core).astype(BF)
        dims = (((0,), (1,)), ((), ()))
        return lax.dot_general(pick, a, dims, preferred_element_type=F32).astype(BF)

    at_other, at_own = shift(grad_rows(1 - c), "c", 1), grad_rows(c)
    n_heads, at_own, at_other = lax.optimization_barrier((n_heads, at_own, at_other))
    grad = near_pair(par, n_heads, head, unit, emb, inv, part)

    part = second_sum(at_other, shift(grad, "c", 1), first_sum(at_own, grad))
    part = lax.all_to_all(part, ("xl", "y", "m"), 0, 0, tiled=False)
    part = jnp.sum(part.reshape(8, 2, 72, HW).astype(F32), axis=0)
    part = part.reshape(2, 8, 9, HW).transpose(1, 0, 2, 3).reshape(8, 18, HW)
    part = lax.all_to_all(part, Z, 0, 0, tiled=False)
    part = jnp.sum(part, axis=0)
    return part[:9, :W], part[9:, :W]


def solution(mesh):
    parts = Mesh(mesh.devices.reshape(SIZES), NAMES)
    batch = ("xl", "z1", "z2", "y", "c")
    in_specs = (
        P(batch, None),
        P(batch, None),
        P(batch, "m"),
        P(batch, "m"),
        P(batch, None),
        P(),
        P(),
    )
    out_specs = (P(batch, "m"), P(batch, "m"))
    return jax.shard_map(local, mesh=parts, in_specs=in_specs, out_specs=out_specs, check_vma=False)
```

```python
import functools

import jax
import jax.numpy as jnp
import numpy as np
from jax import lax
from jax.experimental import pallas as pl
from jax.experimental.pallas import tpu as pltpu
from jax.sharding import Mesh
from jax.sharding import PartitionSpec as P

EPS = 1e-06
LOSS_SHARE = 0.0625
BF = jnp.bfloat16
F32 = jnp.float32

NAMES = ("xl", "z1", "z2", "y", "c", "m")
SIZES = (2, 2, 4, 4, 2, 2)
Z = ("z1", "z2")
W = 576
HW = 640
EW = 2 * HW
F = 1152
TOK = 768
TM = 384
ROWS = 144
STEPS = (0, -1, 1, 2)
CORE = ("xl", "z1", "z2", "c", "m")


def _head_order():
    k = np.arange(F)
    block, r = k // 144, k % 144
    xl, z2 = block // 4, block % 4
    y, z1, c, i = r // 36, (r % 36) // 18, (r % 18) // 9, r % 9
    return ((((xl * 2 + z1) * 4 + z2) * 4 + y) * 2 + c) * 9 + i


def _grad_order():
    s = np.arange(F // 2)
    xl, y, z, i = s // 288, (s % 288) // 72, (s % 72) // 9, s % 9
    return (((xl * 8 + z) * 4 + y) * 2) * 9 + i


def shift_xz(v, by, last):
    pairs = []
    for i in range(64):
        xl, z, c, m = i // 32, i // 4 % 8, i // 2 % 2, i % 2
        x = m * 2 + xl
        if (c == 0) != last:
            x = (x + by) % 4
        else:
            z = (z + by) % 8
        pairs.append((i, (((x % 2) * 8 + z) * 2 + c) * 2 + x // 2))
    return lax.ppermute(v, CORE, pairs)


def shift(v, axis, by):
    n = lax.axis_size(axis)
    return lax.ppermute(v, axis, [(i, (i + by) % n) for i in range(n)])


def to_neighbour(v):
    pairs = [(b * 2 + m, ((b + 1 - 2 * m) % 128) * 2 + m) for b in range(128) for m in range(2)]
    return lax.ppermute(v, NAMES, pairs)


def in_order(mine, other, index):
    return jnp.where(
        index == 0, jnp.concatenate([mine, other], 0), jnp.concatenate([other, mine], 0)
    )


NT = (((1,), (1,)), ((), ()))


def normalized(raw):
    inv_len = 1.0 / jnp.sqrt(jnp.sum(raw * raw, axis=1, keepdims=True) + EPS)
    return raw * inv_len, inv_len


def own_kernel(*refs):
    par, a_hbm, b_hbm, rowkey, colkey = refs[:5]
    pieces = refs[5:21]
    unit, emb, inv, part, head_out = refs[21:26]
    heads, av, bv, bemb, sem = refs[26:]
    m, c = lax.axis_index("m"), lax.axis_index("c")
    x = m * 2 + lax.axis_index("xl")
    z2 = lax.axis_index("z2")
    load_a = pltpu.make_async_copy(a_hbm, av, sem.at[32])
    load_b = pltpu.make_async_copy(b_hbm, bv, sem.at[33])
    copies = []

    def put(src, k, head, first, last):
        dx = jnp.where(head == 0, first, last)
        dz = jnp.where(head == 0, last, first)
        xx = lax.rem(x + dx + 4, 4)
        block = lax.rem(xx, 2) * 4 + lax.rem(z2 + dz + 4, 4)
        copies.append(
            pltpu.make_async_copy(
                src.at[pl.ds(k * ROWS, ROWS)],
                heads.at[
                    head,
                    pl.ds(pl.multiple_of(block * ROWS, 16), ROWS),
                    pl.ds(pl.multiple_of((xx // 2) * HW, 128), HW),
                ],
                sem.at[head * 16 + len(copies) % 16],
            )
        )

    def arrive(head):
        for i in range(16):
            rows = heads.at[head, pl.ds(0, ROWS), pl.ds(0, HW)]
            pltpu.make_async_copy(pieces[0].at[pl.ds(0, ROWS)], rows, sem.at[head * 16 + i]).wait()

    for group in range(2):
        head = c if group == 0 else 1 - c
        for k, last in enumerate((0, -1, 1, 2)):
            near, far = pieces[group * 8 + 2 * k : group * 8 + 2 * k + 2]
            for i, first in enumerate(STEPS):
                put(near if i < 2 else far, i % 2, head, first, last)
    load_a.start()
    for copy in copies:
        copy.start()
    load_b.start()
    load_a.wait()
    arrive(m)

    scale, offset = par[0], par[1]
    gain = scale * LOSS_SHARE
    for t in range(2):
        rows = pl.ds(t * TM, TM)
        u, inv_len = normalized(jnp.dot(av[rows], heads[m], preferred_element_type=F32))
        unit[rows] = u
        emb[rows] = u.astype(BF)
        inv[rows] = jnp.broadcast_to(inv_len, (TM, 128))
    load_b.wait()
    arrive(1 - m)
    save = pltpu.make_async_copy(heads.at[1 - m], head_out, sem.at[34])
    save.start()
    for t in range(2):
        rows = pl.ds(t * TM, TM)
        u, _ = normalized(jnp.dot(bv[rows], heads[1 - m], preferred_element_type=F32))
        bemb[rows] = u.astype(BF)
    for t in range(2):
        rows = pl.ds(t * TM, TM)
        logit = lax.dot_general(emb[rows], bemb[...], NT, preferred_element_type=F32) * scale + offset
        hit = rowkey[rows] == colkey[...]
        coef = jnp.where(hit, -gain, gain) / (1.0 + jnp.exp(jnp.where(hit, logit, -logit)))
        part[rows] = jnp.dot(coef.astype(BF), bemb[...], preferred_element_type=F32)
    save.wait()


def near_kernel(last, *refs):
    if last:
        par, n, head, emb, part, unit, inv, out, nemb = refs
    else:
        par, n, head, emb, part, out, nemb = refs
    scale, offset = par[0], par[1]
    gain = scale * LOSS_SHARE
    u, _ = normalized(jnp.dot(n[...], head[...], preferred_element_type=F32))
    nemb[...] = u.astype(BF)
    for t in range(2):
        rows = pl.ds(t * TM, TM)
        logit = lax.dot_general(emb[rows], nemb[...], NT, preferred_element_type=F32) * scale + offset
        coef = gain / (1.0 + jnp.exp(-logit))
        grad = part[rows] + jnp.dot(coef.astype(BF), nemb[...], preferred_element_type=F32)
        if last:
            u = unit[rows]
            radial = jnp.sum(u * grad, axis=1, keepdims=True)
            out[rows] = ((grad - u * radial) * inv[rows][:, :1]).astype(BF)
        else:
            out[rows] = grad


ANY = pl.BlockSpec(memory_space=pl.ANY)
VM = pl.BlockSpec(memory_space=pltpu.VMEM)
SM = pl.BlockSpec(memory_space=pltpu.SMEM)


def hbm(v):
    return pltpu.with_memory_space_constraint(v, pltpu.HBM)


def vmem(v):
    return pltpu.with_memory_space_constraint(v, pltpu.VMEM)


def own_pair(par, a, b, rowkey, colkey, pieces):
    return pl.pallas_call(
        own_kernel,
        out_shape=(
            pltpu.VMEM((TOK, EW), F32),
            pltpu.VMEM((TOK, EW), BF),
            pltpu.VMEM((TOK, 128), F32),
            pltpu.VMEM((TOK, EW), F32),
            pltpu.VMEM((F, EW), BF),
        ),
        in_specs=[SM, ANY, ANY, VM, VM] + [ANY] * 16,
        out_specs=(VM, VM, VM, VM, VM),
        scratch_shapes=[
            pltpu.VMEM((2, F, EW), BF),
            pltpu.VMEM((TOK, F), BF),
            pltpu.VMEM((TOK, F), BF),
            pltpu.VMEM((TOK, EW), BF),
            pltpu.SemaphoreType.DMA((35,)),
        ],
        compiler_params=pltpu.CompilerParams(vmem_limit_bytes=30 << 20),
        cost_estimate=pl.CostEstimate(flops=7_500_000_000, bytes_accessed=23_000_000, transcendentals=1_200_000),
    )(par, hbm(a), hbm(b), rowkey, colkey, *[hbm(p) for p in pieces])


def near_pair(par, n, head, emb, part, *rest):
    arrays = [vmem(v) for v in (n, head, emb, part, *rest)]
    return pl.pallas_call(
        functools.partial(near_kernel, bool(rest)),
        out_shape=jax.ShapeDtypeStruct((TOK, EW), BF) if rest else pltpu.VMEM((TOK, EW), F32),
        in_specs=[SM] + [VM] * len(arrays),
        out_specs=VM,
        scratch_shapes=[pltpu.VMEM((TOK // 2, EW), BF)],
        compiler_params=pltpu.CompilerParams(vmem_limit_bytes=20 << 20),
        cost_estimate=pl.CostEstimate(flops=2_700_000_000, bytes_accessed=7_000_000, transcendentals=600_000),
    )(par, *arrays)


def first_sum_kernel(at, grad, out):
    @pl.loop(0, 2)
    def _(t):
        rows = pl.ds(pl.multiple_of(t * 288, 288), 288)
        out[rows] = jnp.dot(at[rows], grad[...], preferred_element_type=F32)


def second_sum_kernel(at, grad, part, out):
    @pl.loop(0, 2)
    def _(t):
        rows = pl.ds(pl.multiple_of(t * 288, 288), 288)
        total = part[rows] + jnp.dot(at[rows], grad[...], preferred_element_type=F32)
        for k in range(4):
            for half in range(2):
                out[t * 8 + k * 2 + half] = total[
                    k * 72 : (k + 1) * 72, half * HW : (half + 1) * HW
                ].astype(BF)


def first_sum(at, grad):
    return pl.pallas_call(
        first_sum_kernel,
        out_shape=jax.ShapeDtypeStruct((F // 2, EW), F32),
        compiler_params=pltpu.CompilerParams(vmem_limit_bytes=24 << 20),
        cost_estimate=pl.CostEstimate(flops=1_132_462_080, bytes_accessed=5_800_000, transcendentals=0),
    )(at, grad)


def second_sum(at, grad, part):
    return pl.pallas_call(
        second_sum_kernel,
        out_shape=jax.ShapeDtypeStruct((16, 72, HW), BF),
        compiler_params=pltpu.CompilerParams(vmem_limit_bytes=24 << 20),
        cost_estimate=pl.CostEstimate(flops=1_132_462_080, bytes_accessed=7_000_000, transcendentals=0),
    )(at, grad, part)


def after(value, *others):
    return lax.optimization_barrier((value, *others))[0]


def local(image_feats, text_feats, image_head, text_head, positive, logit_scale, logit_bias):
    m, c = lax.axis_index("m"), lax.axis_index("c")
    z1, y = lax.axis_index("z1"), lax.axis_index("y")

    image_other, text_other = shift(image_head, "c", 1), shift(text_head, "c", 1)
    v = jnp.where(
        c == 0,
        jnp.concatenate([image_head, image_other], 0),
        jnp.concatenate([text_other, text_head], 0),
    )
    v = jnp.pad(in_order(v, shift(v, "z1", 1), z1), ((0, 0), (0, HW - W)))
    got = [v, shift(v, "y", 1), shift(v, "y", -1), shift(v, "y", 2)]
    (images, texts), got = lax.optimization_barrier(((image_feats, text_feats), got))
    v = jnp.zeros((4, 36, HW), BF)
    for by, g in zip((0, 1, -1, 2), got):
        v = lax.dynamic_update_slice(v, g[None], ((y - by + 4) % 4, 0, 0))
    v = v.reshape(ROWS, HW)

    rows = lax.broadcasted_iota(jnp.int32, (F, F), 0)
    to_heads = (rows == jnp.asarray(_head_order(), jnp.int32)[None, :]).astype(BF)
    a = jnp.where(m == 0, images, texts)
    a_heads = jnp.dot(a, to_heads, preferred_element_type=F32).astype(BF)
    lo = jnp.concatenate([v, shift_xz(v, 1, False)], 0)
    far, a_heads = lax.optimization_barrier((shift_xz(v, 2, False), a_heads))
    hi = jnp.concatenate([shift_xz(v, -1, False), far], 0)
    images, texts = after((image_feats, text_feats), hi)
    b = jnp.where(m == 0, texts, images)
    b_heads = jnp.dot(b, to_heads, preferred_element_type=F32).astype(BF)
    lo_left, hi_right = shift_xz(lo, 1, True), shift_xz(hi, -1, True)
    hi_left, lo_right = shift_xz(hi, 1, True), shift_xz(lo, -1, True)
    (lo_left, hi_right), b_heads = lax.optimization_barrier(((lo_left, hi_right), b_heads))
    lo_far, hi_far = shift_xz(lo_left, 1, True), shift_xz(hi_right, -1, True)
    par = jnp.concatenate([logit_scale, logit_bias])
    ident = lax.iota(jnp.int32, TOK)
    rowkey = jnp.where(m == 0, positive[0], ident)[:, None]
    colkey = jnp.where(m == 0, ident, positive[0])[None, :]
    lo, par, rowkey, colkey = lax.optimization_barrier((lo, par, rowkey, colkey))
    own = [lo, hi, lo_left, hi_left, lo_right, hi_right, lo_far, hi_far]
    pieces = own + [shift(p, "c", 1) for p in own]

    half = TOK // 2
    b_first, b_last = after((b_heads[:half], b_heads[half:]), pieces[10], pieces[13])
    n_first = to_neighbour(b_first)
    n_last = to_neighbour(b_last)
    unit, emb, inv, part, head = own_pair(par, a_heads, b_heads, rowkey, colkey, pieces)
    n_first, part = lax.optimization_barrier((n_first, part))
    part = near_pair(par, n_first, head, emb, part)

    a = after(a, part)
    order = jnp.asarray(_grad_order(), jnp.int32)[None, :]

    def grad_rows(core):
        pick = (rows[:, : F // 2] == order + 9 * core).astype(BF)
        dims = (((0,), (1,)), ((), ()))
        return lax.dot_general(pick, a, dims, preferred_element_type=F32).astype(BF)

    at_other, at_own = shift(grad_rows(1 - c), "c", 1), grad_rows(c)
    n_last, at_own, at_other = lax.optimization_barrier((n_last, at_own, at_other))
    grad = near_pair(par, n_last, head, emb, part, unit, inv)

    part = second_sum(at_other, shift(grad, "c", 1), first_sum(at_own, grad))
    part = lax.all_to_all(part, ("xl", "y", "m"), 0, 0, tiled=False)
    part = jnp.sum(part.reshape(8, 2, 72, HW).astype(F32), axis=0)
    part = part.reshape(2, 8, 9, HW).transpose(1, 0, 2, 3).reshape(8, 18, HW)
    part = lax.all_to_all(part, Z, 0, 0, tiled=False)
    part = jnp.sum(part, axis=0)
    return part[:9, :W], part[9:, :W]


def solution(mesh):
    parts = Mesh(mesh.devices.reshape(SIZES), NAMES)
    batch = ("xl", "z1", "z2", "y", "c")
    in_specs = (
        P(batch, None),
        P(batch, None),
        P(batch, "m"),
        P(batch, "m"),
        P(batch, None),
        P(),
        P(),
    )
    out_specs = (P(batch, "m"), P(batch, "m"))
    return jax.shard_map(local, mesh=parts, in_specs=in_specs, out_specs=out_specs, check_vma=False)
```

```python
import functools

import jax
import jax.numpy as jnp
import numpy as np
from jax import lax
from jax.experimental import pallas as pl
from jax.experimental.pallas import tpu as pltpu
from jax.sharding import Mesh
from jax.sharding import PartitionSpec as P

EPS = 1e-06
LOSS_SHARE = 0.0625
BF = jnp.bfloat16
F32 = jnp.float32

NAMES = ("xl", "z1", "z2", "y", "c", "m")
SIZES = (2, 2, 4, 4, 2, 2)
Z = ("z1", "z2")
W = 576
HW = 640
EW = 2 * HW
F = 1152
TOK = 768
TM = 384
ROWS = 144
STEPS = (0, -1, 1, 2)
CORE = ("xl", "z1", "z2", "c", "m")


def _head_order():
    k = np.arange(F)
    block, r = k // 144, k % 144
    xl, z2 = block // 4, block % 4
    y, z1, c, i = r // 36, (r % 36) // 18, (r % 18) // 9, r % 9
    return ((((xl * 2 + z1) * 4 + z2) * 4 + y) * 2 + c) * 9 + i


def _grad_order():
    s = np.arange(F // 2)
    xl, y, z, i = s // 288, (s % 288) // 72, (s % 72) // 9, s % 9
    return (((xl * 8 + z) * 4 + y) * 2) * 9 + i


def shift_xz(v, by, last):
    pairs = []
    for i in range(64):
        xl, z, c, m = i // 32, i // 4 % 8, i // 2 % 2, i % 2
        x = m * 2 + xl
        if (c == 0) != last:
            x = (x + by) % 4
        else:
            z = (z + by) % 8
        pairs.append((i, (((x % 2) * 8 + z) * 2 + c) * 2 + x // 2))
    return lax.ppermute(v, CORE, pairs)


def shift(v, axis, by):
    n = lax.axis_size(axis)
    return lax.ppermute(v, axis, [(i, (i + by) % n) for i in range(n)])


def to_neighbour(v):
    pairs = [(b * 2 + m, ((b + 1 - 2 * m) % 128) * 2 + m) for b in range(128) for m in range(2)]
    return lax.ppermute(v, NAMES, pairs)


def in_order(mine, other, index):
    return jnp.where(
        index == 0, jnp.concatenate([mine, other], 0), jnp.concatenate([other, mine], 0)
    )


NT = (((1,), (1,)), ((), ()))


def normalized(raw):
    inv_len = 1.0 / jnp.sqrt(jnp.sum(raw * raw, axis=1, keepdims=True) + EPS)
    return raw * inv_len, inv_len


def own_kernel(*refs):
    par, a_hbm, b_first, b_last, rowkey, colkey = refs[:6]
    pieces = refs[6:22]
    unit, emb, inv, part, head_out = refs[22:27]
    heads, av, bv, bemb, sem = refs[27:]
    m, c = lax.axis_index("m"), lax.axis_index("c")
    x = m * 2 + lax.axis_index("xl")
    z2 = lax.axis_index("z2")
    load_a = pltpu.make_async_copy(a_hbm, av, sem.at[32])
    load_b = pltpu.make_async_copy(b_first, bv.at[pl.ds(0, TM)], sem.at[33])
    load_c = pltpu.make_async_copy(b_last, bv.at[pl.ds(TM, TM)], sem.at[35])
    copies = []

    def put(src, k, head, first, last):
        dx = jnp.where(head == 0, first, last)
        dz = jnp.where(head == 0, last, first)
        xx = lax.rem(x + dx + 4, 4)
        block = lax.rem(xx, 2) * 4 + lax.rem(z2 + dz + 4, 4)
        copies.append(
            pltpu.make_async_copy(
                src.at[pl.ds(k * ROWS, ROWS)],
                heads.at[
                    head,
                    pl.ds(pl.multiple_of(block * ROWS, 16), ROWS),
                    pl.ds(pl.multiple_of((xx // 2) * HW, 128), HW),
                ],
                sem.at[head * 16 + len(copies) % 16],
            )
        )

    def arrive(head):
        for i in range(16):
            rows = heads.at[head, pl.ds(0, ROWS), pl.ds(0, HW)]
            pltpu.make_async_copy(pieces[0].at[pl.ds(0, ROWS)], rows, sem.at[head * 16 + i]).wait()

    for group in range(2):
        head = c if group == 0 else 1 - c
        for k, last in enumerate((0, -1, 1, 2)):
            near, far = pieces[group * 8 + 2 * k : group * 8 + 2 * k + 2]
            for i, first in enumerate(STEPS):
                put(near if i < 2 else far, i % 2, head, first, last)
    load_a.start()
    for copy in copies:
        copy.start()
    load_b.start()
    load_c.start()
    load_a.wait()
    arrive(m)

    scale, offset = par[0], par[1]
    gain = scale * LOSS_SHARE
    for t in range(2):
        rows = pl.ds(t * TM, TM)
        u, inv_len = normalized(jnp.dot(av[rows], heads[m], preferred_element_type=F32))
        unit[rows] = u
        emb[rows] = u.astype(BF)
        inv[rows] = jnp.broadcast_to(inv_len, (TM, 128))
    load_b.wait()
    load_c.wait()
    arrive(1 - m)
    save = pltpu.make_async_copy(heads.at[1 - m], head_out, sem.at[34])
    save.start()
    for t in range(2):
        rows = pl.ds(t * TM, TM)
        u, _ = normalized(jnp.dot(bv[rows], heads[1 - m], preferred_element_type=F32))
        bemb[rows] = u.astype(BF)
    for t in range(2):
        rows = pl.ds(t * TM, TM)
        logit = lax.dot_general(emb[rows], bemb[...], NT, preferred_element_type=F32) * scale + offset
        hit = rowkey[rows] == colkey[...]
        coef = jnp.where(hit, -gain, gain) / (1.0 + jnp.exp(jnp.where(hit, logit, -logit)))
        part[rows] = jnp.dot(coef.astype(BF), bemb[...], preferred_element_type=F32)
    save.wait()


def near_kernel(last, *refs):
    if last:
        par, n, head, emb, part, unit, inv, out, nemb = refs
    else:
        par, n, head, emb, part, out, nemb = refs
    scale, offset = par[0], par[1]
    gain = scale * LOSS_SHARE
    u, _ = normalized(jnp.dot(n[...], head[...], preferred_element_type=F32))
    nemb[...] = u.astype(BF)
    for t in range(2):
        rows = pl.ds(t * TM, TM)
        logit = lax.dot_general(emb[rows], nemb[...], NT, preferred_element_type=F32) * scale + offset
        coef = gain / (1.0 + jnp.exp(-logit))
        grad = part[rows] + jnp.dot(coef.astype(BF), nemb[...], preferred_element_type=F32)
        if last:
            u = unit[rows]
            radial = jnp.sum(u * grad, axis=1, keepdims=True)
            out[rows] = ((grad - u * radial) * inv[rows][:, :1]).astype(BF)
        else:
            out[rows] = grad


ANY = pl.BlockSpec(memory_space=pl.ANY)
VM = pl.BlockSpec(memory_space=pltpu.VMEM)
SM = pl.BlockSpec(memory_space=pltpu.SMEM)


def hbm(v):
    return pltpu.with_memory_space_constraint(v, pltpu.HBM)


def vmem(v):
    return pltpu.with_memory_space_constraint(v, pltpu.VMEM)


def own_pair(par, a, b_first, b_last, rowkey, colkey, pieces):
    return pl.pallas_call(
        own_kernel,
        out_shape=(
            pltpu.VMEM((TOK, EW), F32),
            pltpu.VMEM((TOK, EW), BF),
            pltpu.VMEM((TOK, 128), F32),
            pltpu.VMEM((TOK, EW), F32),
            pltpu.VMEM((F, EW), BF),
        ),
        in_specs=[SM, ANY, ANY, ANY, VM, VM] + [ANY] * 16,
        out_specs=(VM, VM, VM, VM, VM),
        scratch_shapes=[
            pltpu.VMEM((2, F, EW), BF),
            pltpu.VMEM((TOK, F), BF),
            pltpu.VMEM((TOK, F), BF),
            pltpu.VMEM((TOK, EW), BF),
            pltpu.SemaphoreType.DMA((36,)),
        ],
        compiler_params=pltpu.CompilerParams(vmem_limit_bytes=30 << 20),
        cost_estimate=pl.CostEstimate(flops=7_500_000_000, bytes_accessed=23_000_000, transcendentals=1_200_000),
    )(par, hbm(a), hbm(b_first), hbm(b_last), rowkey, colkey, *[hbm(p) for p in pieces])


def near_pair(par, n, head, emb, part, *rest):
    arrays = [vmem(v) for v in (n, head, emb, part, *rest)]
    return pl.pallas_call(
        functools.partial(near_kernel, bool(rest)),
        out_shape=jax.ShapeDtypeStruct((TOK, EW), BF) if rest else pltpu.VMEM((TOK, EW), F32),
        in_specs=[SM] + [VM] * len(arrays),
        out_specs=VM,
        scratch_shapes=[pltpu.VMEM((TOK // 2, EW), BF)],
        compiler_params=pltpu.CompilerParams(vmem_limit_bytes=20 << 20),
        cost_estimate=pl.CostEstimate(flops=2_700_000_000, bytes_accessed=7_000_000, transcendentals=600_000),
    )(par, *arrays)


def first_sum_kernel(at, grad, out):
    @pl.loop(0, 2)
    def _(t):
        rows = pl.ds(pl.multiple_of(t * 288, 288), 288)
        out[rows] = jnp.dot(at[rows], grad[...], preferred_element_type=F32)


def second_sum_kernel(at, grad, part, out):
    @pl.loop(0, 2)
    def _(t):
        rows = pl.ds(pl.multiple_of(t * 288, 288), 288)
        total = part[rows] + jnp.dot(at[rows], grad[...], preferred_element_type=F32)
        for k in range(4):
            for half in range(2):
                out[t * 8 + k * 2 + half] = total[
                    k * 72 : (k + 1) * 72, half * HW : (half + 1) * HW
                ].astype(BF)


def first_sum(at, grad):
    return pl.pallas_call(
        first_sum_kernel,
        out_shape=jax.ShapeDtypeStruct((F // 2, EW), F32),
        compiler_params=pltpu.CompilerParams(vmem_limit_bytes=24 << 20),
        cost_estimate=pl.CostEstimate(flops=1_132_462_080, bytes_accessed=5_800_000, transcendentals=0),
    )(at, grad)


def second_sum(at, grad, part):
    return pl.pallas_call(
        second_sum_kernel,
        out_shape=jax.ShapeDtypeStruct((16, 72, HW), BF),
        compiler_params=pltpu.CompilerParams(vmem_limit_bytes=24 << 20),
        cost_estimate=pl.CostEstimate(flops=1_132_462_080, bytes_accessed=7_000_000, transcendentals=0),
    )(at, grad, part)


def after(value, *others):
    return lax.optimization_barrier((value, *others))[0]


def local(image_feats, text_feats, image_head, text_head, positive, logit_scale, logit_bias):
    m, c = lax.axis_index("m"), lax.axis_index("c")
    z1, y = lax.axis_index("z1"), lax.axis_index("y")

    image_other, text_other = shift(image_head, "c", 1), shift(text_head, "c", 1)
    v = jnp.where(
        c == 0,
        jnp.concatenate([image_head, image_other], 0),
        jnp.concatenate([text_other, text_head], 0),
    )
    par = jnp.concatenate([logit_scale, logit_bias])
    ident = lax.iota(jnp.int32, TOK)
    at = after(positive[0], v)
    rowkey = jnp.where(m == 0, at, ident)[:, None]
    colkey = jnp.where(m == 0, ident, at)[None, :]
    v = jnp.pad(in_order(v, shift(v, "z1", 1), z1), ((0, 0), (0, HW - W)))
    v, par, rowkey, colkey = lax.optimization_barrier((v, par, rowkey, colkey))
    got = [v, shift(v, "y", 1), shift(v, "y", -1), shift(v, "y", 2)]
    (images, texts), got = lax.optimization_barrier(((image_feats, text_feats), got))
    v = jnp.zeros((4, 36, HW), BF)
    for by, g in zip((0, 1, -1, 2), got):
        v = lax.dynamic_update_slice(v, g[None], ((y - by + 4) % 4, 0, 0))
    v = v.reshape(ROWS, HW)

    rows = lax.broadcasted_iota(jnp.int32, (F, F), 0)
    to_heads = (rows == jnp.asarray(_head_order(), jnp.int32)[None, :]).astype(BF)
    a = jnp.where(m == 0, images, texts)
    a_heads = jnp.dot(a, to_heads, preferred_element_type=F32).astype(BF)
    lo = jnp.concatenate([v, shift_xz(v, 1, False)], 0)
    far, a_heads = lax.optimization_barrier((shift_xz(v, 2, False), a_heads))
    hi = jnp.concatenate([shift_xz(v, -1, False), far], 0)
    images, texts = after((image_feats, text_feats), hi)
    b = jnp.where(m == 0, texts, images)
    b_heads = tuple(
        jnp.dot(b[k : k + TM], to_heads, preferred_element_type=F32).astype(BF) for k in (0, TM)
    )
    lo_left, hi_right = shift_xz(lo, 1, True), shift_xz(hi, -1, True)
    hi_left, lo_right = shift_xz(hi, 1, True), shift_xz(lo, -1, True)
    (lo_left, hi_right), b_heads = lax.optimization_barrier(((lo_left, hi_right), b_heads))
    lo_far, hi_far = shift_xz(lo_left, 1, True), shift_xz(hi_right, -1, True)
    own = [lo, hi, lo_left, hi_left, lo_right, hi_right, lo_far, hi_far]
    pieces = own + [shift(p, "c", 1) for p in own]

    b_first, b_last = after(b_heads, pieces[10], pieces[13])
    n_first = to_neighbour(b_first)
    n_last = to_neighbour(b_last)
    unit, emb, inv, part, head = own_pair(par, a_heads, b_first, b_last, rowkey, colkey, pieces)
    n_first, part = lax.optimization_barrier((n_first, part))
    part = near_pair(par, n_first, head, emb, part)

    a = after(a, part)
    order = jnp.asarray(_grad_order(), jnp.int32)[None, :]

    def grad_rows(core):
        pick = (rows[:, : F // 2] == order + 9 * core).astype(BF)
        dims = (((0,), (1,)), ((), ()))
        return lax.dot_general(pick, a, dims, preferred_element_type=F32).astype(BF)

    at_other, at_own = shift(grad_rows(1 - c), "c", 1), grad_rows(c)
    n_last, at_own, at_other = lax.optimization_barrier((n_last, at_own, at_other))
    grad = near_pair(par, n_last, head, emb, part, unit, inv)

    part = second_sum(at_other, shift(grad, "c", 1), first_sum(at_own, grad))
    part = lax.all_to_all(part, ("xl", "y", "m"), 0, 0, tiled=False)
    part = jnp.sum(part.reshape(8, 2, 72, HW).astype(F32), axis=0)
    part = part.reshape(2, 8, 9, HW).transpose(1, 0, 2, 3).reshape(8, 18, HW)
    part = lax.all_to_all(part, Z, 0, 0, tiled=False)
    part = jnp.sum(part, axis=0)
    return part[:9, :W], part[9:, :W]


def solution(mesh):
    parts = Mesh(mesh.devices.reshape(SIZES), NAMES)
    batch = ("xl", "z1", "z2", "y", "c")
    in_specs = (
        P(batch, None),
        P(batch, None),
        P(batch, "m"),
        P(batch, "m"),
        P(batch, None),
        P(),
        P(),
    )
    out_specs = (P(batch, "m"), P(batch, "m"))
    return jax.shard_map(local, mesh=parts, in_specs=in_specs, out_specs=out_specs, check_vma=False)
```
